256 devices in a mesh: row: 32 (over z_hi, y, core), col: 8 (over z_lo, x).
Axes of the slice: x: 4, y: 4, z: 8 (z_hi: 4, z_lo: 2; z = z_hi * 2 + z_lo), core: 2. Of those that a mesh axis runs over, the one named last changes fastest.
Arguments:
- kernel: float32 [4, 32, 128, 16, 8, 128], P(None, 'row', None, None, 'col'), may hold values from 0 to 20
Outputs:
- factored: float32 [4, 32, 128, 16, 8, 128], P(None, 'row', None, None, 'col')
The draws below stay inside these ranges and needn't reach their ends.
All inputs are finite; a program needn't handle non-finite values.
Results may differ from the reference program's by a relative error of at most 0.00006.
Values sent between devices are 32-bit elements; how exact they have to be, the bound alone decides.
No kernel may reach another device: no remote copies, remote signals or barrier semaphores. Data moves between devices by JAX's collectives and lax.ppermute only.
A program may use at most 64 MiB of HBM per device.

```python
import math
import jax
import jax.numpy as jnp
from jax import lax

BLK = 128
RB_DEV = 4
CB_DEV = 16
ORDER = 16384


def draw_kernel(key, part):
    key = jax.random.fold_in(key, 11)
    key_one, key_two, key_three = jax.random.split(key, 3)
    coords = jax.random.uniform(key_one, (ORDER, 8), jnp.float32)
    length = 0.5
    scales = jnp.exp(jax.random.uniform(key_two, (ORDER,), jnp.float32, math.log(0.5), math.log(2.0)))
    nugget = jax.random.uniform(key_three, (ORDER,), jnp.float32, 0.5, 2.0)
    squared = jnp.zeros((ORDER, ORDER), jnp.float32)
    for feature in range(8):
        offset = coords[:, feature][:, None] - coords[:, feature][None, :]
        squared = squared + offset * offset
    values = jnp.exp(-jnp.sqrt(squared) / length)
    same_point = jnp.arange(ORDER)[:, None] == jnp.arange(ORDER)[None, :]
    values = values + jnp.where(same_point, nugget[:, None], 0.0)
    values = values * scales[:, None] * scales[None, :]
    grid_rows = ORDER // (RB_DEV * BLK)
    grid_cols = ORDER // (CB_DEV * BLK)
    return values.reshape(RB_DEV, grid_rows, BLK, CB_DEV, grid_cols, BLK).astype(jnp.float32)


def setup_inputs(seed: int = 0) -> dict:
    seeds = jax.random.split(jax.random.key(seed), 2)
    kernel = draw_kernel(jax.random.fold_in(seeds[1], 71), 0)
    return dict(kernel=kernel)


def reference(kernel):
    full_order = kernel.shape[0] * kernel.shape[1] * kernel.shape[2]
    panel_size = 2 * kernel.shape[2]
    matrix = kernel.reshape(full_order, full_order)
    factor = jnp.linalg.cholesky(matrix[:panel_size, :panel_size])
    below_panel = lax.linalg.triangular_solve(factor, matrix[panel_size:, :panel_size].T, left_side=True, lower=True).T
    trailing = matrix[panel_size:, panel_size:] - jnp.dot(below_panel, below_panel.T, precision=lax.Precision.HIGHEST)
    top_part = jnp.concatenate([factor, below_panel.T], 1)
    bottom = jnp.concatenate([below_panel, trailing], 1)
    return jnp.concatenate([top_part, bottom], 0).reshape(kernel.shape)
```

```python
import functools

import jax
import jax.numpy as jnp
from jax import lax
from jax.experimental import pallas as pl
from jax.experimental.pallas import tpu as pltpu
from jax.sharding import PartitionSpec as P

HIGHEST = lax.Precision.HIGHEST
BLK = 128
PANEL = 2 * BLK
AXES = ("row", "col")


def device_id(zh, y, core, zl, x):
    return ((zh % 4) * 8 + (y % 4) * 2 + core) * 8 + zl * 4 + x % 4


def all_places():
    for zh in range(4):
        for y in range(4):
            for core in range(2):
                for zl in range(2):
                    for x in range(4):
                        yield zh, y, core, zl, x


def send(value, target):
    pairs = []
    for place in all_places():
        to = target(*place)
        if to is not None:
            pairs.append((device_id(*place), device_id(*to)))
    return lax.ppermute(value, AXES, pairs)


def dot_nt(a, b):
    return lax.dot_general(
        a, b, (((1,), (1,)), ((), ())), precision=HIGHEST, preferred_element_type=jnp.float32
    )


def dot_tn(a, b):
    return lax.dot_general(
        a, b, (((0,), (0,)), ((), ())), precision=HIGHEST, preferred_element_type=jnp.float32
    )


def dot_nn(a, b):
    return lax.dot_general(
        a, b, (((1,), (0,)), ((), ())), precision=HIGHEST, preferred_element_type=jnp.float32
    )


def factor_kernel(nb, d00_ref, d01_ref, d11_ref, u_ref, w_ref, m_ref):
    lane = lax.broadcasted_iota(jnp.int32, (nb, BLK), 1)
    sub = lax.broadcasted_iota(jnp.int32, (nb, BLK), 0)
    for p in range(PANEL // nb):
        k0 = p * nb
        half = k0 // BLK
        c0 = k0 % BLK
        if half == 0:
            tiles = [d00_ref[k0 : k0 + nb, :], d01_ref[k0 : k0 + nb, :]]
        else:
            tiles = [None, d11_ref[c0 : c0 + nb, :]]
        for t in range(2):
            one = jnp.where(lane + t * BLK == sub + k0, 1.0, 0.0)
            tiles.append(one if t <= half else None)
        if p > 0:
            lhs = m_ref[0:k0, k0 : k0 + nb]
            for t in range(4):
                if tiles[t] is not None:
                    tiles[t] = tiles[t] - dot_tn(lhs, m_ref[0:k0, t * BLK : (t + 1) * BLK])
        spread = [
            jnp.broadcast_to(tiles[half][:, c0 + j : c0 + j + 1], (nb, BLK)) for j in range(nb)
        ]
        pivots = jnp.ones((nb, BLK), jnp.float32)
        for k in range(nb):
            column = spread[k]
            pivot = jnp.broadcast_to(column[k : k + 1, :], (nb, BLK))
            pivots = jnp.where(sub == k, pivot, pivots)
            if k < nb - 1:
                ratio = jnp.where(sub > k, column, 0.0) * (1.0 / pivot)
                for j in range(k + 1, nb):
                    spread[j] = spread[j] - ratio * jnp.broadcast_to(column[j : j + 1, :], (nb, BLK))
                for t in range(4):
                    if tiles[t] is not None:
                        tiles[t] = tiles[t] - ratio * jnp.broadcast_to(
                            tiles[t][k : k + 1, :], (nb, BLK)
                        )
        scale = lax.rsqrt(pivots)
        for t in range(4):
            if tiles[t] is None:
                out = jnp.zeros((nb, BLK), jnp.float32)
            else:
                out = tiles[t] * scale
                if t == half:
                    out = jnp.where(lane >= sub + c0, out, 0.0)
            m_ref[k0 : k0 + nb, t * BLK : (t + 1) * BLK] = out
    u_ref[...] = m_ref[:, :PANEL]
    w_ref[...] = m_ref[:, PANEL:]


def factorize(d00, d01, d11):
    square = jax.ShapeDtypeStruct((PANEL, PANEL), jnp.float32)
    vmem = pl.BlockSpec(memory_space=pltpu.VMEM)
    return pl.pallas_call(
        functools.partial(factor_kernel, 32),
        out_shape=[square, square],
        in_specs=[vmem] * 3,
        out_specs=[vmem] * 2,
        scratch_shapes=[pltpu.VMEM((PANEL, 2 * PANEL), jnp.float32)],
        compiler_params=pltpu.CompilerParams(vmem_limit_bytes=24 * 1024 * 1024),
        cost_estimate=pl.CostEstimate(flops=10000000, bytes_accessed=800000, transcendentals=0),
        name="factorize",
    )(d00, d01, d11)


def update_kernel(rows, pos_ref, a_ref, near_ref, far_ref, *refs):
    mine = refs[0:4]
    other = refs[4:8]
    wnear_ref, wfar_ref, wmine_ref, wother_ref, u_ref, o_ref, top_ref, left_ref = refs[8:]
    step = pl.program_id(0)
    row, col = pos_ref[0], pos_ref[1]
    y, zh = pos_ref[2], pos_ref[3]

    @pl.when(step == 0)
    def _():
        left_ref[...] = dot_nt(near_ref[...], wnear_ref[...]) + dot_nt(far_ref[...], wfar_ref[...])
        for d in range(4):
            top_ref[:, d * 512 : (d + 1) * 512] = dot_nt(wmine_ref[...], mine[d][...]) + dot_nt(
                wother_ref[...], other[d][...]
            )

    lhs = left_ref[pl.ds(pl.multiple_of(step * rows, rows), rows), :]
    for n in range(8):
        product = dot_nn(lhs, top_ref[:, n * 256 : (n + 1) * 256])
        for h in range(2):
            slot = 2 * n + h
            j = 4 * lax.rem(y + slot // 4, 4) + lax.rem(zh + slot % 4, 4)
            at = pl.ds(j, rows, 16)
            o_ref[at, :] = a_ref[at, :] - product[:, h * BLK : (h + 1) * BLK]

    @pl.when((row < 2) & (step == 0))
    def _():
        first = pl.ds(pl.multiple_of(row * BLK, BLK), BLK)
        for slot in range(16):
            j = 4 * lax.rem(y + slot // 4, 4) + lax.rem(zh + slot % 4, 4)
            o_ref[pl.ds(j, BLK, 16), :] = top_ref[first, slot * BLK : (slot + 1) * BLK]

    @pl.when(col < 2)
    def _():
        wide = left_ref[pl.ds(pl.multiple_of(step * rows, rows), rows), :]
        o_ref[pl.ds(0, rows, 16), :] = jnp.where(col == 0, wide[:, :BLK], wide[:, BLK:])

    @pl.when((row < 2) & (col < 2) & (step == 0))
    def _():
        strip = u_ref[pl.ds(pl.multiple_of(col * BLK, BLK), BLK), :]
        o_ref[pl.ds(0, BLK, 16), :] = jnp.where(row == 0, strip[:, :BLK], strip[:, BLK:]).T


def update(pos, a, near, far, mine, other, wnear, wfar, wmine, wother, upper):
    rows = BLK
    vmem = pl.BlockSpec(memory_space=pltpu.VMEM)
    tile = pl.BlockSpec((rows * 16, BLK), lambda i: (i, 0))
    return pl.pallas_call(
        functools.partial(update_kernel, rows),
        grid=(4,),
        out_shape=jax.ShapeDtypeStruct(a.shape, jnp.float32),
        in_specs=[pl.BlockSpec(memory_space=pltpu.SMEM), tile] + [vmem] * 15,
        out_specs=tile,
        scratch_shapes=[
            pltpu.VMEM((PANEL, 2048), jnp.float32),
            pltpu.VMEM((512, PANEL), jnp.float32),
        ],
        compiler_params=pltpu.CompilerParams(vmem_limit_bytes=40 * 1024 * 1024),
        cost_estimate=pl.CostEstimate(
            flops=5000000000, bytes_accessed=12000000, transcendentals=0
        ),
        name="update",
    )(pos, a, near, far, *mine, *other, wnear, wfar, wmine, wother, upper)


def local(kernel):
    row = lax.axis_index("row")
    col = lax.axis_index("col")
    zh, y, core = row // 8, (row // 2) % 4, row % 2
    x = col % 4
    flat = kernel.reshape(512 * 16, BLK)
    left = kernel.reshape(4, BLK, 16, BLK)[:, :, 0, :]

    with jax.named_scope("diag"):
        block = left[0]
        d00 = send(block, lambda zh, y, core, zl, x: (0, 0, 0, 0, 1) if (zh, y, core, zl, x) == (0, 0, 0, 0, 0) else None)
        d01 = send(block[64:], lambda zh, y, core, zl, x: (0, 0, 1, 0, 1) if (zh, y, core, zl, x) == (0, 0, 0, 0, 1) else None)
        packed = jnp.where(
            core == 0, jnp.concatenate([d00, block[:64]]), jnp.concatenate([d01, block])
        )
        packed = jnp.where((row < 2) & (col == 1), packed, 0.0)
        got = [
            send(packed, lambda zh, y, core, zl, x, s=s: (0, 0, core, 0, x + s) if (zh, y, zl, x) == (0, 0, 0, 1) else None)
            for s in (1, 3, 2)
        ]
        packed = packed + got[0] + got[1] + got[2]
        got = [
            send(packed, lambda zh, y, core, zl, x, s=s: (0, y + s, core, 0, x) if (zh, y, zl) == (0, 0, 0) else None)
            for s in (1, 3, 2)
        ]
        packed = packed + got[0] + got[1] + got[2]
        got = [
            send(packed, lambda zh, y, core, zl, x, s=s: (zh + s, y, core, 0, x) if (zh, zl) == (0, 0) else None)
            for s in (1, 3, 2)
        ]
        packed = packed + got[0] + got[1] + got[2]
        got = send(packed, lambda zh, y, core, zl, x: (zh, y, core, 1, x) if zl == 0 else None)
        packed = packed + got
        swapped = send(packed, lambda zh, y, core, zl, x: (zh, y, 1 - core, zl, x))
        first = jnp.where(core == 0, packed, swapped)
        second = jnp.where(core == 0, swapped, packed)
        upper, inverse = factorize(
            first[:128], jnp.concatenate([first[128:], second[:64]]), second[64:]
        )

    with jax.named_scope("rows"):
        r1 = send(left, lambda zh, y, core, zl, x: (zh, y, core, 0, 3 - x) if zl == 0 and x < 2 else None)
        r2 = send(left, lambda zh, y, core, zl, x: (zh, y, core, 1, x) if zl == 0 and x < 2 else None)
        r3 = send(r2, lambda zh, y, core, zl, x: (zh, y, core, 1, 3 - x) if zl == 1 and x < 2 else None)
        near = jnp.where(col < 2, left, 0.0) + r1 + r2 + r3
        far = send(near, lambda zh, y, core, zl, x: (zh, y, core, zl, x ^ 1))

    with jax.named_scope("cols"):
        piece = None
        for s in range(4):
            part = lax.dynamic_index_in_dim(left, (y + s) % 4, 0, keepdims=False)
            got = send(
                part,
                lambda zh, y, core, zl, x, s=s: (zh, y + s, x, y // 2, 2 * (y % 2) + core)
                if zl == 0 and x < 2
                else None,
            )
            piece = got if piece is None else piece + got
        over_z = [piece] + [
            send(piece, lambda zh, y, core, zl, x, s=s: (zh - s, y, core, zl, x)) for s in (1, 2, 3)
        ]
        own = jnp.concatenate([v[None] for v in over_z])
        up = send(own, lambda zh, y, core, zl, x: (zh, y - 1, core, zl, x))
        down = send(own, lambda zh, y, core, zl, x: (zh, y + 1, core, zl, x))
        opposite = jnp.concatenate(
            [
                send(down[:2], lambda zh, y, core, zl, x: (zh, y + 1, core, zl, x)),
                send(up[2:], lambda zh, y, core, zl, x: (zh, y - 1, core, zl, x)),
            ]
        )
        mine = [own, up, opposite, down]
        other = [send(v, lambda zh, y, core, zl, x: (zh, y, 1 - core, zl, x)) for v in mine]

    with jax.named_scope("final"):
        lo, hi = inverse[:, :BLK], inverse[:, BLK:]
        near_is_lo = (x == 0) | (x == 3)
        wnear, wfar = jnp.where(near_is_lo, lo, hi), jnp.where(near_is_lo, hi, lo)
        wmine, wother = jnp.where(core == 0, lo, hi), jnp.where(core == 0, hi, lo)
        pos = jnp.stack([row, col, y, zh]).astype(jnp.int32)
        tall = lambda v: v.reshape(512, BLK)
        out = update(
            pos, flat, tall(near), tall(far), [tall(v) for v in mine], [tall(v) for v in other],
            wnear, wfar, wmine, wother, upper,
        )
    return out.reshape(kernel.shape)


def solution(mesh):
    placed = P(None, "row", None, None, "col", None)
    return jax.shard_map(
        local, mesh=mesh, in_specs=(placed,), out_specs=placed, check_vma=False
    )
```

```python
import functools

import jax
import jax.numpy as jnp
from jax import lax
from jax.experimental import pallas as pl
from jax.experimental.pallas import tpu as pltpu
from jax.sharding import PartitionSpec as P

HIGHEST = lax.Precision.HIGHEST
BLK = 128
PANEL = 2 * BLK
AXES = ("row", "col")


def device_id(zh, y, core, zl, x):
    return ((zh % 4) * 8 + (y % 4) * 2 + core) * 8 + zl * 4 + x % 4


def all_places():
    for zh in range(4):
        for y in range(4):
            for core in range(2):
                for zl in range(2):
                    for x in range(4):
                        yield zh, y, core, zl, x


def pairs_of(target):
    pairs = {}
    for place in all_places():
        to = target(*place)
        if to is not None:
            pairs[device_id(*place)] = device_id(*to)
    return pairs


def closed(pairs):
    source = {to: at for at, to in pairs.items()}
    out = dict(pairs)
    for end in source:
        if end not in pairs:
            start = end
            while start in source:
                start = source[start]
            out[end] = start
    used = set(out) | set(out.values())
    for at in range(256):
        sibling = at ^ 8
        if at not in used and sibling not in used:
            out[at] = sibling
    return sorted(out.items())


def send(value, target):
    return lax.ppermute(value, AXES, closed(pairs_of(target)))


def spread(which, value, payloads, targets):
    got = [send(p, t) for p, t in zip(payloads, targets)]
    for i, v in enumerate(got):
        value = v if value is None else jnp.where(which == i + 1, v, value)
    return value


def dot(a, b, contract):
    return lax.dot_general(a, b, (contract, ((), ())), preferred_element_type=jnp.float32)


def dot_tn(a, b):
    return lax.dot_general(
        a, b, (((0,), (0,)), ((), ())), precision=HIGHEST, preferred_element_type=jnp.float32
    )


def halves(v):
    high = v.astype(jnp.bfloat16)
    return high, (v - high.astype(jnp.float32)).astype(jnp.bfloat16)


def dot_pairs(pairs):
    left, right = [], []
    for a, b in pairs:
        ah, al = halves(a)
        bh, bl = halves(b)
        left += [ah, ah, al]
        right += [bh, bl, bh]
    return dot(jnp.concatenate(left, 1), jnp.concatenate(right, 1), ((1,), (1,)))


def prepare_kernel(pos_ref, a_ref, left_ref, p0_ref, p1_ref, p2_ref, p3_ref):
    left_ref[...] = a_ref[:, 0, :]
    y = pos_ref[2]
    for s, p_ref in enumerate((p0_ref, p1_ref, p2_ref, p3_ref)):
        block = lax.rem(y + s, 4)
        p_ref[...] = left_ref[pl.ds(pl.multiple_of(block * BLK, BLK), BLK), :]


def prepare(pos, a):
    vmem = pl.BlockSpec(memory_space=pltpu.VMEM)
    block = jax.ShapeDtypeStruct((BLK, BLK), jnp.float32)
    return pl.pallas_call(
        prepare_kernel,
        grid=(1,),
        out_shape=[jax.ShapeDtypeStruct((512, BLK), jnp.float32)] + [block] * 4,
        in_specs=[
            pl.BlockSpec(memory_space=pltpu.SMEM),
            pl.BlockSpec((512, 8, BLK), lambda i: (0, 0, 0)),
        ],
        out_specs=[vmem] * 5,
        compiler_params=pltpu.CompilerParams(vmem_limit_bytes=24 * 1024 * 1024),
        name="prepare",
    )(pos, a.reshape(512, 16, BLK))

def factor_kernel(nb, pos_ref, own_ref, across_ref, core_ref, both_ref, u_ref, w_ref, m_ref, d00_ref, d01_ref, d11_ref):
    even, low = pos_ref[4] == 0, pos_ref[5] == 1
    left_mine = jnp.where(low, own_ref[...], across_ref[...])
    right_mine = jnp.where(low, across_ref[...], own_ref[...])
    left_other = jnp.where(low, core_ref[...], both_ref[...])
    right_other = jnp.where(low, both_ref[...], core_ref[...])
    d00_ref[...] = jnp.where(even, left_mine, left_other)
    d01_ref[...] = jnp.where(even, right_mine, right_other)
    d11_ref[...] = jnp.where(even, right_other, right_mine)
    lane = lax.broadcasted_iota(jnp.int32, (nb, BLK), 1)
    sub = lax.broadcasted_iota(jnp.int32, (nb, BLK), 0)
    for p in range(PANEL // nb):
        k0 = p * nb
        half = k0 // BLK
        c0 = k0 % BLK
        if half == 0:
            tiles = [d00_ref[k0 : k0 + nb, :], d01_ref[k0 : k0 + nb, :]]
        else:
            tiles = [None, d11_ref[c0 : c0 + nb, :]]
        for t in range(2):
            one = jnp.where(lane + t * BLK == sub + k0, 1.0, 0.0)
            tiles.append(one if t <= half else None)
        if p > 0:
            lhs = m_ref[0:k0, k0 : k0 + nb]
            for t in range(4):
                if tiles[t] is not None:
                    tiles[t] = tiles[t] - dot_tn(lhs, m_ref[0:k0, t * BLK : (t + 1) * BLK])
        spread = [
            jnp.broadcast_to(tiles[half][:, c0 + j : c0 + j + 1], (nb, BLK)) for j in range(nb)
        ]
        pivots = jnp.ones((nb, BLK), jnp.float32)
        for k in range(nb):
            column = spread[k]
            pivot = jnp.broadcast_to(column[k : k + 1, :], (nb, BLK))
            pivots = jnp.where(sub == k, pivot, pivots)
            if k < nb - 1:
                ratio = jnp.where(sub > k, column, 0.0) * (1.0 / pivot)
                for j in range(k + 1, nb):
                    spread[j] = spread[j] - ratio * jnp.broadcast_to(column[j : j + 1, :], (nb, BLK))
                for t in range(4):
                    if tiles[t] is not None:
                        tiles[t] = tiles[t] - ratio * jnp.broadcast_to(
                            tiles[t][k : k + 1, :], (nb, BLK)
                        )
        scale = lax.rsqrt(pivots)
        for t in range(4):
            if tiles[t] is None:
                out = jnp.zeros((nb, BLK), jnp.float32)
            else:
                out = tiles[t] * scale
                if t == half:
                    out = jnp.where(lane >= sub + c0, out, 0.0)
            m_ref[k0 : k0 + nb, t * BLK : (t + 1) * BLK] = out
    u_ref[...] = m_ref[:, :PANEL]
    w_ref[...] = m_ref[:, PANEL:]


def factorize(pos, own, across, core, both):
    square = jax.ShapeDtypeStruct((PANEL, PANEL), jnp.float32)
    vmem = pl.BlockSpec(memory_space=pltpu.VMEM)
    return pl.pallas_call(
        functools.partial(factor_kernel, 32),
        out_shape=[square, square],
        in_specs=[pl.BlockSpec(memory_space=pltpu.SMEM)] + [vmem] * 4,
        out_specs=[vmem] * 2,
        scratch_shapes=[pltpu.VMEM((PANEL, 2 * PANEL), jnp.float32)]
        + [pltpu.VMEM((BLK, BLK), jnp.float32)] * 3,
        compiler_params=pltpu.CompilerParams(vmem_limit_bytes=24 * 1024 * 1024),
        cost_estimate=pl.CostEstimate(flops=4000000000, bytes_accessed=800000, transcendentals=0),
        name="factorize",
    )(pos, own, across, core, both)


def update_kernel(rows, pos_ref, a_ref, near_ref, far_ref, *refs):
    mine = refs[0:4]
    other = refs[4:8]
    w_ref, u_ref, o_ref = refs[8:11]
    thigh_ref, tlow_ref, shigh_ref, slow_ref, top_ref, left_ref, sum_ref = refs[11:]
    step = pl.program_id(0)
    row, col, y, zh = pos_ref[0], pos_ref[1], pos_ref[2], pos_ref[3]
    even, low = pos_ref[4] == 0, pos_ref[5] == 1

    @pl.when(step == 0)
    def _():
        wlo, whi = w_ref[:, :BLK], w_ref[:, BLK:]
        wnear, wfar = jnp.where(low, wlo, whi), jnp.where(low, whi, wlo)
        solved = dot_pairs([(near_ref[...], wnear), (far_ref[...], wfar)])
        shigh_ref[...], slow_ref[...] = halves(solved)
        left_ref[...] = jnp.where(col == 0, solved[:, :BLK], solved[:, BLK:])
        wmine, wother = jnp.where(even, wlo, whi), jnp.where(even, whi, wlo)
        for d in range(4):
            solved = dot_pairs([(wmine, mine[d][...]), (wother, other[d][...])])
            high, lower = halves(solved)
            for k in range(4):
                j = 4 * lax.rem(y + d, 4) + lax.rem(zh + k, 4)
                at = pl.ds(pl.multiple_of(j * BLK, BLK), BLK)
                thigh_ref[:, at] = high[:, k * BLK : (k + 1) * BLK]
                tlow_ref[:, at] = lower[:, k * BLK : (k + 1) * BLK]

                @pl.when(row < 2)
                def _():
                    block = solved[:, k * BLK : (k + 1) * BLK]
                    top_ref[:, at] = jnp.where(row == 0, block[:BLK], block[BLK:])

    at = pl.ds(pl.multiple_of(step * rows, rows), rows)
    shigh, slow = shigh_ref[at, :], slow_ref[at, :]
    wide = jnp.concatenate([shigh, shigh, slow], 1)
    for n in range(8):
        cut = slice(n * 256, (n + 1) * 256)
        thigh, tlow = thigh_ref[:, cut], tlow_ref[:, cut]
        sum_ref[:, cut] = dot(wide, jnp.concatenate([thigh, tlow, thigh], 0), ((1,), (0,)))
    o_ref[...] = a_ref[...] - sum_ref[...].reshape(rows, 16, BLK).reshape(rows * 16, BLK)

    @pl.when((row < 2) & (step == 0))
    def _():
        o_ref[: BLK * 16, :] = top_ref[...].reshape(BLK, 16, BLK).reshape(BLK * 16, BLK)

    @pl.when(col < 2)
    def _():
        o_ref[pl.ds(0, rows, 16), :] = left_ref[at, :]

    @pl.when((row < 2) & (col < 2) & (step == 0))
    def _():
        strip = u_ref[pl.ds(pl.multiple_of(col * BLK, BLK), BLK), :]
        o_ref[pl.ds(0, BLK, 16), :] = jnp.where(row == 0, strip[:, :BLK], strip[:, BLK:]).T


def update(pos, a, near, far, mine, other, inverse, upper):
    rows = 2 * BLK
    vmem = pl.BlockSpec(memory_space=pltpu.VMEM)
    tile = pl.BlockSpec((rows * 16, BLK), lambda i: (i, 0))
    return pl.pallas_call(
        functools.partial(update_kernel, rows),
        grid=(512 // rows,),
        out_shape=jax.ShapeDtypeStruct(a.shape, jnp.float32),
        in_specs=[pl.BlockSpec(memory_space=pltpu.SMEM), tile] + [vmem] * 12,
        out_specs=tile,
        scratch_shapes=[
            pltpu.VMEM((PANEL, 2048), jnp.bfloat16),
            pltpu.VMEM((PANEL, 2048), jnp.bfloat16),
            pltpu.VMEM((512, PANEL), jnp.bfloat16),
            pltpu.VMEM((512, PANEL), jnp.bfloat16),
            pltpu.VMEM((BLK, 2048), jnp.float32),
            pltpu.VMEM((512, BLK), jnp.float32),
            pltpu.VMEM((rows, 2048), jnp.float32),
        ],
        compiler_params=pltpu.CompilerParams(vmem_limit_bytes=40 * 1024 * 1024),
        cost_estimate=pl.CostEstimate(
            flops=3000000000, bytes_accessed=12000000, transcendentals=0
        ),
        name="update",
    )(pos, a, near, far, *mine, *other, inverse, upper)


def local(kernel):
    row = lax.axis_index("row")
    col = lax.axis_index("col")
    zh, y, core = row // 8, (row // 2) % 4, row % 2
    zl, x = col // 4, col % 4
    low = (x == 0) | (x == 3)
    pos = jnp.stack([row, col, y, zh, core, low.astype(row.dtype)]).astype(jnp.int32)
    flat = kernel.reshape(512 * 16, BLK)
    left, p0, p1, p2, p3 = prepare(pos, flat)

    with jax.named_scope("rows"):
        held = spread(zl, left, [left], [lambda zh, y, core, zl, x: (zh, y, core, 1, x) if zl == 0 and x < 2 else None])
        near = spread(x >> 1, held, [held], [lambda zh, y, core, zl, x: (zh, y, core, zl, 3 - x) if x < 2 else None])

    with jax.named_scope("diag"):
        diag = left[:BLK]
        root = lambda zh, y, zl, x: (zh, y, zl) == (0, 0, 0) and x < 2
        stages = [
            [
                lambda zh, y, core, zl, x, t=t, m=m: (0, 0, core, t, 3 - x if m else x) if root(zh, y, zl, x) else None
                for t, m in ((0, True), (1, False), (1, True))
            ],
            [
                lambda zh, y, core, zl, x, s=s: (0, y + s, core, zl, x) if (zh, y) == (0, 0) else None
                for s in (1, 3, 2)
            ],
            [
                lambda zh, y, core, zl, x, s=s: (zh + s, y, core, zl, x) if zh == 0 else None
                for s in (1, 3, 2)
            ],
        ]
        near_pair = (x >> 1) + 2 * zl
        arrivals = [
            jnp.where((zh == 0) & (y == 0), near_pair, 0),
            jnp.where(zh == 0, jnp.where(y == 0, 0, jnp.where(y == 1, 1, jnp.where(y == 3, 2, 3))), 0),
            jnp.where(zh == 0, 0, jnp.where(zh == 1, 1, jnp.where(zh == 3, 2, 3))),
        ]
        for which, targets in zip(arrivals, stages):
            diag = spread(which, diag, [diag] * 3, targets)
        diag, near = lax.optimization_barrier((diag, near))
        across = send(diag, lambda zh, y, core, zl, x: (zh, y, core, zl, x ^ 1))
        both = send(diag, lambda zh, y, core, zl, x: (zh, y, 1 - core, zl, x ^ 1))
        cored = send(diag, lambda zh, y, core, zl, x: (zh, y, 1 - core, zl, x))
        far = send(near, lambda zh, y, core, zl, x: (zh, y, core, zl, x ^ 1))
        upper, inverse = factorize(pos, diag, across, cored, both)

    with jax.named_scope("cols"):
        piece = spread(
            lax.rem(y - (col >> 1) + 4, 4) + 1,
            None,
            [p0, p1, p2, p3],
            [
                lambda zh, y, core, zl, x, s=s: (zh, y + s, x, y // 2, 2 * (y % 2) + core)
                if zl == 0 and x < 2
                else None
                for s in range(4)
            ],
        )
        over_z = [piece] + [
            send(piece, lambda zh, y, core, zl, x, s=s: (zh - s, y, core, zl, x)) for s in (1, 2, 3)
        ]
        own = jnp.concatenate(over_z)
        around = [
            send(own, lambda zh, y, core, zl, x, s=s: (zh, y - s, core, zl, x)) for s in (1, 2, 3)
        ]
        *around, inverse = lax.optimization_barrier((*around, inverse))
        mine = [own] + around
        other = [send(v, lambda zh, y, core, zl, x: (zh, y, 1 - core, zl, x)) for v in mine]

    with jax.named_scope("final"):
        out = update(pos, flat, near, far, mine, other, inverse, upper)
    return out.reshape(kernel.shape)


def solution(mesh):
    placed = P(None, "row", None, None, "col", None)
    return jax.shard_map(
        local, mesh=mesh, in_specs=(placed,), out_specs=placed, check_vma=False
    )
```

```python
import functools

import jax
import jax.numpy as jnp
from jax import lax
from jax.experimental import pallas as pl
from jax.experimental.pallas import tpu as pltpu
from jax.sharding import PartitionSpec as P

HIGHEST = lax.Precision.HIGHEST
BLK = 128
PANEL = 2 * BLK
AXES = ("row", "col")


def device_id(zh, y, core, zl, x):
    return ((zh % 4) * 8 + (y % 4) * 2 + core) * 8 + zl * 4 + x % 4


def all_places():
    for zh in range(4):
        for y in range(4):
            for core in range(2):
                for zl in range(2):
                    for x in range(4):
                        yield zh, y, core, zl, x


def pairs_of(target):
    pairs = {}
    for place in all_places():
        to = target(*place)
        if to is not None:
            pairs[device_id(*place)] = device_id(*to)
    return pairs


def closed(pairs):
    source = {to: at for at, to in pairs.items()}
    out = dict(pairs)
    for end in source:
        if end not in pairs:
            start = end
            while start in source:
                start = source[start]
            out[end] = start
    used = set(out) | set(out.values())
    for at in range(256):
        sibling = at ^ 8
        if at not in used and sibling not in used:
            out[at] = sibling
    return sorted(out.items())


def send(value, target):
    return lax.ppermute(value, AXES, closed(pairs_of(target)))


def spread(which, value, payloads, targets):
    got = [send(p, t) for p, t in zip(payloads, targets)]
    for i, v in enumerate(got):
        value = v if value is None else jnp.where(which == i + 1, v, value)
    return value


def dot(a, b, contract):
    return lax.dot_general(a, b, (contract, ((), ())), preferred_element_type=jnp.float32)


def dot_tn(a, b):
    return lax.dot_general(
        a, b, (((0,), (0,)), ((), ())), precision=HIGHEST, preferred_element_type=jnp.float32
    )


def halves(v):
    high = v.astype(jnp.bfloat16)
    return high, (v - high.astype(jnp.float32)).astype(jnp.bfloat16)


def dot_pairs(pairs):
    left, right = [], []
    for a, b in pairs:
        ah, al = halves(a)
        bh, bl = halves(b)
        left += [ah, ah, al]
        right += [bh, bl, bh]
    return dot(jnp.concatenate(left, 1), jnp.concatenate(right, 1), ((1,), (1,)))


def prepare_kernel(pos_ref, a_ref, left_ref, p0_ref, p1_ref, p2_ref, p3_ref):
    left_ref[...] = a_ref[:, 0, :]
    y = pos_ref[2]
    for s, p_ref in enumerate((p0_ref, p1_ref, p2_ref, p3_ref)):
        block = lax.rem(y + s, 4)
        p_ref[...] = left_ref[pl.ds(pl.multiple_of(block * BLK, BLK), BLK), :]


def prepare(pos, a):
    vmem = pl.BlockSpec(memory_space=pltpu.VMEM)
    block = jax.ShapeDtypeStruct((BLK, BLK), jnp.float32)
    return pl.pallas_call(
        prepare_kernel,
        grid=(1,),
        out_shape=[jax.ShapeDtypeStruct((512, BLK), jnp.float32)] + [block] * 4,
        in_specs=[
            pl.BlockSpec(memory_space=pltpu.SMEM),
            pl.BlockSpec((512, 8, BLK), lambda i: (0, 0, 0)),
        ],
        out_specs=[vmem] * 5,
        compiler_params=pltpu.CompilerParams(vmem_limit_bytes=24 * 1024 * 1024),
        name="prepare",
    )(pos, a.reshape(512, 16, BLK))

def factor_kernel(nb, pos_ref, own_ref, across_ref, core_ref, both_ref, u_ref, w_ref, m_ref, d00_ref, d01_ref, d11_ref):
    even, low = pos_ref[4] == 0, pos_ref[5] == 1
    left_mine = jnp.where(low, own_ref[...], across_ref[...])
    right_mine = jnp.where(low, across_ref[...], own_ref[...])
    left_other = jnp.where(low, core_ref[...], both_ref[...])
    right_other = jnp.where(low, both_ref[...], core_ref[...])
    d00_ref[...] = jnp.where(even, left_mine, left_other)
    d01_ref[...] = jnp.where(even, right_mine, right_other)
    d11_ref[...] = jnp.where(even, right_other, right_mine)
    lane = lax.broadcasted_iota(jnp.int32, (nb, BLK), 1)
    sub = lax.broadcasted_iota(jnp.int32, (nb, BLK), 0)
    for p in range(PANEL // nb):
        k0 = p * nb
        half = k0 // BLK
        c0 = k0 % BLK
        if half == 0:
            tiles = [d00_ref[k0 : k0 + nb, :], d01_ref[k0 : k0 + nb, :]]
        else:
            tiles = [None, d11_ref[c0 : c0 + nb, :]]
        for t in range(2):
            one = jnp.where(lane + t * BLK == sub + k0, 1.0, 0.0)
            tiles.append(one if t <= half else None)
        if p > 0:
            lhs = m_ref[0:k0, k0 : k0 + nb]
            for t in range(4):
                if tiles[t] is not None:
                    tiles[t] = tiles[t] - dot_tn(lhs, m_ref[0:k0, t * BLK : (t + 1) * BLK])
        spread = [
            jnp.broadcast_to(tiles[half][:, c0 + j : c0 + j + 1], (nb, BLK)) for j in range(nb)
        ]
        pivots = jnp.ones((nb, BLK), jnp.float32)
        for k in range(nb):
            column = spread[k]
            pivot = jnp.broadcast_to(column[k : k + 1, :], (nb, BLK))
            pivots = jnp.where(sub == k, pivot, pivots)
            if k < nb - 1:
                ratio = jnp.where(sub > k, column, 0.0) * (1.0 / pivot)
                for j in range(k + 1, nb):
                    spread[j] = spread[j] - ratio * jnp.broadcast_to(column[j : j + 1, :], (nb, BLK))
                for t in range(4):
                    if tiles[t] is not None:
                        tiles[t] = tiles[t] - ratio * jnp.broadcast_to(
                            tiles[t][k : k + 1, :], (nb, BLK)
                        )
        scale = lax.rsqrt(pivots)
        for t in range(4):
            if tiles[t] is None:
                out = jnp.zeros((nb, BLK), jnp.float32)
            else:
                out = tiles[t] * scale
                if t == half:
                    out = jnp.where(lane >= sub + c0, out, 0.0)
            m_ref[k0 : k0 + nb, t * BLK : (t + 1) * BLK] = out
    u_ref[...] = m_ref[:, :PANEL]
    w_ref[...] = m_ref[:, PANEL:]


def factorize(pos, own, across, core, both):
    square = jax.ShapeDtypeStruct((PANEL, PANEL), jnp.float32)
    vmem = pl.BlockSpec(memory_space=pltpu.VMEM)
    return pl.pallas_call(
        functools.partial(factor_kernel, 32),
        out_shape=[square, square],
        in_specs=[pl.BlockSpec(memory_space=pltpu.SMEM)] + [vmem] * 4,
        out_specs=[vmem] * 2,
        scratch_shapes=[pltpu.VMEM((PANEL, 2 * PANEL), jnp.float32)]
        + [pltpu.VMEM((BLK, BLK), jnp.float32)] * 3,
        compiler_params=pltpu.CompilerParams(vmem_limit_bytes=24 * 1024 * 1024),
        cost_estimate=pl.CostEstimate(flops=4000000000, bytes_accessed=800000, transcendentals=0),
        name="factorize",
    )(pos, own, across, core, both)


def early_kernel(pos_ref, near_ref, far_ref, mine_ref, other_ref, w_ref, s_ref, t_ref):
    even, low = pos_ref[4] == 0, pos_ref[5] == 1
    wlo, whi = w_ref[:, :BLK], w_ref[:, BLK:]
    wnear, wfar = jnp.where(low, wlo, whi), jnp.where(low, whi, wlo)
    s_ref[...] = dot_pairs([(near_ref[...], wnear), (far_ref[...], wfar)])
    wmine, wother = jnp.where(even, wlo, whi), jnp.where(even, whi, wlo)
    t_ref[...] = dot_pairs([(wmine, mine_ref[...]), (wother, other_ref[...])])


def solve_early(pos, near, far, mine, other, inverse):
    vmem = pl.BlockSpec(memory_space=pltpu.VMEM)
    return pl.pallas_call(
        early_kernel,
        out_shape=[
            jax.ShapeDtypeStruct((512, PANEL), jnp.float32),
            jax.ShapeDtypeStruct((PANEL, 512), jnp.float32),
        ],
        in_specs=[pl.BlockSpec(memory_space=pltpu.SMEM)] + [vmem] * 5,
        out_specs=[vmem] * 2,
        compiler_params=pltpu.CompilerParams(vmem_limit_bytes=24 * 1024 * 1024),
        cost_estimate=pl.CostEstimate(flops=1000000000, bytes_accessed=3000000, transcendentals=0),
        name="solve_early",
    )(pos, near, far, mine, other, inverse)


def sides_kernel(pos_ref, up_ref, up_other_ref, down_ref, down_other_ref, w_ref, up_t_ref, down_t_ref):
    even = pos_ref[4] == 0
    wlo, whi = w_ref[:, :BLK], w_ref[:, BLK:]
    wmine, wother = jnp.where(even, wlo, whi), jnp.where(even, whi, wlo)
    up_t_ref[...] = dot_pairs([(wmine, up_ref[...]), (wother, up_other_ref[...])])
    down_t_ref[...] = dot_pairs([(wmine, down_ref[...]), (wother, down_other_ref[...])])


def solve_sides(pos, up, up_other, down, down_other, inverse):
    vmem = pl.BlockSpec(memory_space=pltpu.VMEM)
    return pl.pallas_call(
        sides_kernel,
        out_shape=[jax.ShapeDtypeStruct((PANEL, 512), jnp.float32)] * 2,
        in_specs=[pl.BlockSpec(memory_space=pltpu.SMEM)] + [vmem] * 5,
        out_specs=[vmem] * 2,
        compiler_params=pltpu.CompilerParams(vmem_limit_bytes=24 * 1024 * 1024),
        cost_estimate=pl.CostEstimate(flops=1000000000, bytes_accessed=3000000, transcendentals=0),
        name="solve_sides",
    )(pos, up, up_other, down, down_other, inverse)


def update_kernel(rows, pos_ref, a_ref, *refs):
    s_ref, own_ref, up_ref, down_ref, mine_ref, other_ref = refs[0:6]
    w_ref, u_ref, o_ref = refs[6:9]
    thigh_ref, tlow_ref, top_ref, sum_ref = refs[9:]
    step = pl.program_id(0)
    row, col, y, zh = pos_ref[0], pos_ref[1], pos_ref[2], pos_ref[3]
    even = pos_ref[4] == 0

    @pl.when(step == 0)
    def _():
        wlo, whi = w_ref[:, :BLK], w_ref[:, BLK:]
        wmine, wother = jnp.where(even, wlo, whi), jnp.where(even, whi, wlo)
        for d in range(4):
            if d == 2:
                solved = dot_pairs([(wmine, mine_ref[...]), (wother, other_ref[...])])
            else:
                solved = (own_ref, up_ref, None, down_ref)[d][...]
            high, lower = halves(solved)
            for k in range(4):
                j = 4 * lax.rem(y + d, 4) + lax.rem(zh + k, 4)
                at = pl.ds(pl.multiple_of(j * BLK, BLK), BLK)
                thigh_ref[:, at] = high[:, k * BLK : (k + 1) * BLK]
                tlow_ref[:, at] = lower[:, k * BLK : (k + 1) * BLK]

                @pl.when(row < 2)
                def _():
                    block = solved[:, k * BLK : (k + 1) * BLK]
                    top_ref[:, at] = jnp.where(row == 0, block[:BLK], block[BLK:])

    at = pl.ds(pl.multiple_of(step * rows, rows), rows)
    solved_rows = s_ref[at, :]
    shigh, slow = halves(solved_rows)
    wide = jnp.concatenate([shigh, shigh, slow], 1)
    for n in range(8):
        cut = slice(n * 256, (n + 1) * 256)
        thigh, tlow = thigh_ref[:, cut], tlow_ref[:, cut]
        sum_ref[:, cut] = dot(wide, jnp.concatenate([thigh, tlow, thigh], 0), ((1,), (0,)))
    o_ref[...] = a_ref[...] - sum_ref[...].reshape(rows, 16, BLK).reshape(rows * 16, BLK)

    @pl.when((row < 2) & (step == 0))
    def _():
        o_ref[: BLK * 16, :] = top_ref[...].reshape(BLK, 16, BLK).reshape(BLK * 16, BLK)

    @pl.when(col < 2)
    def _():
        o_ref[pl.ds(0, rows, 16), :] = jnp.where(
            col == 0, solved_rows[:, :BLK], solved_rows[:, BLK:]
        )

    @pl.when((row < 2) & (col < 2) & (step == 0))
    def _():
        strip = u_ref[pl.ds(pl.multiple_of(col * BLK, BLK), BLK), :]
        o_ref[pl.ds(0, BLK, 16), :] = jnp.where(row == 0, strip[:, :BLK], strip[:, BLK:]).T


def update(pos, a, early, mine, other, inverse, upper):
    rows = 2 * BLK
    vmem = pl.BlockSpec(memory_space=pltpu.VMEM)
    tile = pl.BlockSpec((rows * 16, BLK), lambda i: (i, 0))
    return pl.pallas_call(
        functools.partial(update_kernel, rows),
        grid=(512 // rows,),
        out_shape=jax.ShapeDtypeStruct(a.shape, jnp.float32),
        in_specs=[pl.BlockSpec(memory_space=pltpu.SMEM), tile] + [vmem] * 8,
        out_specs=tile,
        scratch_shapes=[
            pltpu.VMEM((PANEL, 2048), jnp.bfloat16),
            pltpu.VMEM((PANEL, 2048), jnp.bfloat16),
            pltpu.VMEM((BLK, 2048), jnp.float32),
            pltpu.VMEM((rows, 2048), jnp.float32),
        ],
        compiler_params=pltpu.CompilerParams(vmem_limit_bytes=40 * 1024 * 1024),
        cost_estimate=pl.CostEstimate(
            flops=3000000000, bytes_accessed=12000000, transcendentals=0
        ),
        name="update",
    )(pos, a, *early, mine, other, inverse, upper)


def local(kernel):
    row = lax.axis_index("row")
    col = lax.axis_index("col")
    zh, y, core = row // 8, (row // 2) % 4, row % 2
    zl, x = col // 4, col % 4
    low = (x == 0) | (x == 3)
    pos = jnp.stack([row, col, y, zh, core, low.astype(row.dtype)]).astype(jnp.int32)
    flat = kernel.reshape(512 * 16, BLK)
    left, p0, p1, p2, p3 = prepare(pos, flat)

    with jax.named_scope("rows"):
        held = spread(zl, left, [left], [lambda zh, y, core, zl, x: (zh, y, core, 1, x) if zl == 0 and x < 2 else None])
        near = spread(x >> 1, held, [held], [lambda zh, y, core, zl, x: (zh, y, core, zl, 3 - x) if x < 2 else None])

    with jax.named_scope("diag"):
        diag = left[:BLK]
        root = lambda zh, y, zl, x: (zh, y, zl) == (0, 0, 0) and x < 2
        stages = [
            [
                lambda zh, y, core, zl, x, t=t, m=m: (0, 0, core, t, 3 - x if m else x) if root(zh, y, zl, x) else None
                for t, m in ((0, True), (1, False), (1, True))
            ],
            [
                lambda zh, y, core, zl, x, s=s: (0, y + s, core, zl, x) if (zh, y) == (0, 0) else None
                for s in (1, 3, 2)
            ],
            [
                lambda zh, y, core, zl, x, s=s: (zh + s, y, core, zl, x) if zh == 0 else None
                for s in (1, 3, 2)
            ],
        ]
        near_pair = (x >> 1) + 2 * zl
        arrivals = [
            jnp.where((zh == 0) & (y == 0), near_pair, 0),
            jnp.where(zh == 0, jnp.where(y == 0, 0, jnp.where(y == 1, 1, jnp.where(y == 3, 2, 3))), 0),
            jnp.where(zh == 0, 0, jnp.where(zh == 1, 1, jnp.where(zh == 3, 2, 3))),
        ]
        for which, targets in zip(arrivals, stages):
            diag = spread(which, diag, [diag] * 3, targets)
        diag, near = lax.optimization_barrier((diag, near))
        across = send(diag, lambda zh, y, core, zl, x: (zh, y, core, zl, x ^ 1))
        both = send(diag, lambda zh, y, core, zl, x: (zh, y, 1 - core, zl, x ^ 1))
        cored = send(diag, lambda zh, y, core, zl, x: (zh, y, 1 - core, zl, x))
        far = send(near, lambda zh, y, core, zl, x: (zh, y, core, zl, x ^ 1))
        upper, inverse = factorize(pos, diag, across, cored, both)

    with jax.named_scope("cols"):
        piece = spread(
            lax.rem(y - (col >> 1) + 4, 4) + 1,
            None,
            [p0, p1, p2, p3],
            [
                lambda zh, y, core, zl, x, s=s: (zh, y + s, x, y // 2, 2 * (y % 2) + core)
                if zl == 0 and x < 2
                else None
                for s in range(4)
            ],
        )
        over_z = [piece] + [
            send(piece, lambda zh, y, core, zl, x, s=s: (zh - s, y, core, zl, x)) for s in (1, 2, 3)
        ]
        own = jnp.concatenate(over_z)
        halfway = send(own, lambda zh, y, core, zl, x: (zh, y - 2, core, zl, x))
        around = [
            send(own, lambda zh, y, core, zl, x: (zh, y - 1, core, zl, x)),
            halfway,
            send(own, lambda zh, y, core, zl, x: (zh, y - 3, core, zl, x)),
        ]
        swap = lambda zh, y, core, zl, x: (zh, y, 1 - core, zl, x)
        own_other = send(own, swap)
        up, down, inverse = lax.optimization_barrier((around[0], around[2], inverse))
        other = [own_other, send(up, swap), None, send(down, swap)]
        early = solve_early(pos, near, far, own, own_other, inverse)
        opposite, *early = lax.optimization_barrier((around[1], *early))
        other[2] = send(opposite, swap)
        sides = solve_sides(pos, up, other[1], down, other[3], inverse)

    with jax.named_scope("final"):
        out = update(pos, flat, [*early, *sides], opposite, other[2], inverse, upper)
    return out.reshape(kernel.shape)


def solution(mesh):
    placed = P(None, "row", None, None, "col", None)
    return jax.shard_map(
        local, mesh=mesh, in_specs=(placed,), out_specs=placed, check_vma=False
    )
```

```python
import functools

import jax
import jax.numpy as jnp
from jax import lax
from jax.experimental import pallas as pl
from jax.experimental.pallas import tpu as pltpu
from jax.sharding import PartitionSpec as P

HIGHEST = lax.Precision.HIGHEST
BLK = 128
PANEL = 2 * BLK
AXES = ("row", "col")


def device_id(zh, y, core, zl, x):
    return ((zh % 4) * 8 + (y % 4) * 2 + core) * 8 + zl * 4 + x % 4


def all_places():
    for zh in range(4):
        for y in range(4):
            for core in range(2):
                for zl in range(2):
                    for x in range(4):
                        yield zh, y, core, zl, x


def pairs_of(target):
    pairs = {}
    for place in all_places():
        to = target(*place)
        if to is not None:
            pairs[device_id(*place)] = device_id(*to)
    return pairs


def closed(pairs):
    source = {to: at for at, to in pairs.items()}
    out = dict(pairs)
    for end in source:
        if end not in pairs:
            start = end
            while start in source:
                start = source[start]
            out[end] = start
    used = set(out) | set(out.values())
    for at in range(256):
        sibling = at ^ 8
        if at not in used and sibling not in used:
            out[at] = sibling
    return sorted(out.items())


def send(value, target):
    return lax.ppermute(value, AXES, closed(pairs_of(target)))


def spread(which, value, payloads, targets):
    got = [send(p, t) for p, t in zip(payloads, targets)]
    for i, v in enumerate(got):
        value = v if value is None else jnp.where(which == i + 1, v, value)
    return value


def dot(a, b, contract):
    return lax.dot_general(a, b, (contract, ((), ())), preferred_element_type=jnp.float32)


def dot_tn(a, b):
    return lax.dot_general(
        a, b, (((0,), (0,)), ((), ())), precision=HIGHEST, preferred_element_type=jnp.float32
    )


def halves(v):
    high = v.astype(jnp.bfloat16)
    return high, (v - high.astype(jnp.float32)).astype(jnp.bfloat16)


def dot_pairs(pairs):
    left, right = [], []
    for a, b in pairs:
        ah, al = halves(a)
        bh, bl = halves(b)
        left += [ah, ah, al]
        right += [bh, bl, bh]
    return dot(jnp.concatenate(left, 1), jnp.concatenate(right, 1), ((1,), (1,)))


def prepare_kernel(pos_ref, a_ref, left_ref, p0_ref, p1_ref, p2_ref, p3_ref):
    left_ref[...] = a_ref[:, 0, :]
    y = pos_ref[2]
    for s, p_ref in enumerate((p0_ref, p1_ref, p2_ref, p3_ref)):
        block = lax.rem(y + s, 4)
        p_ref[...] = left_ref[pl.ds(pl.multiple_of(block * BLK, BLK), BLK), :]


def prepare(pos, a):
    vmem = pl.BlockSpec(memory_space=pltpu.VMEM)
    block = jax.ShapeDtypeStruct((BLK, BLK), jnp.float32)
    return pl.pallas_call(
        prepare_kernel,
        grid=(1,),
        out_shape=[jax.ShapeDtypeStruct((512, BLK), jnp.float32)] + [block] * 4,
        in_specs=[
            pl.BlockSpec(memory_space=pltpu.SMEM),
            pl.BlockSpec((512, 8, BLK), lambda i: (0, 0, 0)),
        ],
        out_specs=[vmem] * 5,
        compiler_params=pltpu.CompilerParams(vmem_limit_bytes=24 * 1024 * 1024),
        name="prepare",
    )(pos, a.reshape(512, 16, BLK))

def factor_kernel(nb, pos_ref, own_ref, across_ref, core_ref, both_ref, u_ref, w_ref, m_ref, d00_ref, d01_ref, d11_ref):
    even, low = pos_ref[4] == 0, pos_ref[5] == 1
    left_mine = jnp.where(low, own_ref[...], across_ref[...])
    right_mine = jnp.where(low, across_ref[...], own_ref[...])
    left_other = jnp.where(low, core_ref[...], both_ref[...])
    right_other = jnp.where(low, both_ref[...], core_ref[...])
    d00_ref[...] = jnp.where(even, left_mine, left_other)
    d01_ref[...] = jnp.where(even, right_mine, right_other)
    d11_ref[...] = jnp.where(even, right_other, right_mine)
    lane = lax.broadcasted_iota(jnp.int32, (nb, BLK), 1)
    sub = lax.broadcasted_iota(jnp.int32, (nb, BLK), 0)
    for p in range(PANEL // nb):
        k0 = p * nb
        half = k0 // BLK
        c0 = k0 % BLK
        if half == 0:
            tiles = [d00_ref[k0 : k0 + nb, :], d01_ref[k0 : k0 + nb, :]]
        else:
            tiles = [None, d11_ref[c0 : c0 + nb, :]]
        for t in range(2):
            one = jnp.where(lane + t * BLK == sub + k0, 1.0, 0.0)
            tiles.append(one if t <= half else None)
        if p > 0:
            lhs = m_ref[0:k0, k0 : k0 + nb]
            for t in range(4):
                if tiles[t] is not None:
                    tiles[t] = tiles[t] - dot_tn(lhs, m_ref[0:k0, t * BLK : (t + 1) * BLK])
        spread = [
            jnp.broadcast_to(tiles[half][:, c0 + j : c0 + j + 1], (nb, BLK)) for j in range(nb)
        ]
        pivots = jnp.ones((nb, BLK), jnp.float32)
        for k in range(nb):
            column = spread[k]
            pivot = jnp.broadcast_to(column[k : k + 1, :], (nb, BLK))
            pivots = jnp.where(sub == k, pivot, pivots)
            if k < nb - 1:
                ratio = jnp.where(sub > k, column, 0.0) * (1.0 / pivot)
                for j in range(k + 1, nb):
                    spread[j] = spread[j] - ratio * jnp.broadcast_to(column[j : j + 1, :], (nb, BLK))
                for t in range(4):
                    if tiles[t] is not None:
                        tiles[t] = tiles[t] - ratio * jnp.broadcast_to(
                            tiles[t][k : k + 1, :], (nb, BLK)
                        )
        scale = lax.rsqrt(pivots)
        for t in range(4):
            if tiles[t] is None:
                out = jnp.zeros((nb, BLK), jnp.float32)
            else:
                out = tiles[t] * scale
                if t == half:
                    out = jnp.where(lane >= sub + c0, out, 0.0)
            m_ref[k0 : k0 + nb, t * BLK : (t + 1) * BLK] = out
    u_ref[...] = m_ref[:, :PANEL]
    w_ref[...] = m_ref[:, PANEL:]


def factorize(pos, own, across, core, both):
    square = jax.ShapeDtypeStruct((PANEL, PANEL), jnp.float32)
    vmem = pl.BlockSpec(memory_space=pltpu.VMEM)
    return pl.pallas_call(
        functools.partial(factor_kernel, 32),
        out_shape=[square, square],
        in_specs=[pl.BlockSpec(memory_space=pltpu.SMEM)] + [vmem] * 4,
        out_specs=[vmem] * 2,
        scratch_shapes=[pltpu.VMEM((PANEL, 2 * PANEL), jnp.float32)]
        + [pltpu.VMEM((BLK, BLK), jnp.float32)] * 3,
        compiler_params=pltpu.CompilerParams(vmem_limit_bytes=24 * 1024 * 1024),
        cost_estimate=pl.CostEstimate(flops=4000000000, bytes_accessed=800000, transcendentals=0),
        name="factorize",
    )(pos, own, across, core, both)


def early_kernel(pos_ref, near_ref, far_ref, mine_ref, other_ref, w_ref, s_ref, t_ref):
    even, low = pos_ref[4] == 0, pos_ref[5] == 1
    wlo, whi = w_ref[:, :BLK], w_ref[:, BLK:]
    wnear, wfar = jnp.where(low, wlo, whi), jnp.where(low, whi, wlo)
    s_ref[...] = dot_pairs([(near_ref[...], wnear), (far_ref[...], wfar)])
    wmine, wother = jnp.where(even, wlo, whi), jnp.where(even, whi, wlo)
    t_ref[...] = dot_pairs([(wmine, mine_ref[...]), (wother, other_ref[...])])


def solve_early(pos, near, far, mine, other, inverse):
    vmem = pl.BlockSpec(memory_space=pltpu.VMEM)
    return pl.pallas_call(
        early_kernel,
        out_shape=[
            jax.ShapeDtypeStruct((512, PANEL), jnp.float32),
            jax.ShapeDtypeStruct((PANEL, 512), jnp.float32),
        ],
        in_specs=[pl.BlockSpec(memory_space=pltpu.SMEM)] + [vmem] * 5,
        out_specs=[vmem] * 2,
        compiler_params=pltpu.CompilerParams(vmem_limit_bytes=24 * 1024 * 1024),
        cost_estimate=pl.CostEstimate(flops=1000000000, bytes_accessed=3000000, transcendentals=0),
        name="solve_early",
    )(pos, near, far, mine, other, inverse)


def sides_kernel(pos_ref, up_ref, up_other_ref, down_ref, down_other_ref, w_ref, up_t_ref, down_t_ref):
    even = pos_ref[4] == 0
    wlo, whi = w_ref[:, :BLK], w_ref[:, BLK:]
    wmine, wother = jnp.where(even, wlo, whi), jnp.where(even, whi, wlo)
    up_t_ref[...] = dot_pairs([(wmine, up_ref[...]), (wother, up_other_ref[...])])
    down_t_ref[...] = dot_pairs([(wmine, down_ref[...]), (wother, down_other_ref[...])])


def solve_sides(pos, up, up_other, down, down_other, inverse):
    vmem = pl.BlockSpec(memory_space=pltpu.VMEM)
    return pl.pallas_call(
        sides_kernel,
        out_shape=[jax.ShapeDtypeStruct((PANEL, 512), jnp.float32)] * 2,
        in_specs=[pl.BlockSpec(memory_space=pltpu.SMEM)] + [vmem] * 5,
        out_specs=[vmem] * 2,
        compiler_params=pltpu.CompilerParams(vmem_limit_bytes=24 * 1024 * 1024),
        cost_estimate=pl.CostEstimate(flops=1000000000, bytes_accessed=3000000, transcendentals=0),
        name="solve_sides",
    )(pos, up, up_other, down, down_other, inverse)


def update_kernel(rows, pos_ref, a_ref, *refs):
    s_ref, own_ref, up_ref, down_ref, mine_ref, other_ref = refs[0:6]
    w_ref, u_ref, o_ref = refs[6:9]
    thigh_ref, tlow_ref, top_ref, sum_ref = refs[9:]
    step = pl.program_id(0)
    row, col, y, zh = pos_ref[0], pos_ref[1], pos_ref[2], pos_ref[3]
    even = pos_ref[4] == 0

    @pl.when(step == 0)
    def _():
        wlo, whi = w_ref[:, :BLK], w_ref[:, BLK:]
        wmine, wother = jnp.where(even, wlo, whi), jnp.where(even, whi, wlo)
        for d in range(4):
            if d == 2:
                solved = dot_pairs([(wmine, mine_ref[...]), (wother, other_ref[...])])
            else:
                solved = (own_ref, up_ref, None, down_ref)[d][...]
            high, lower = halves(solved)
            for k in range(4):
                j = 4 * lax.rem(y + d, 4) + lax.rem(zh + k, 4)
                at = pl.ds(pl.multiple_of(j * BLK, BLK), BLK)
                thigh_ref[:, at] = high[:, k * BLK : (k + 1) * BLK]
                tlow_ref[:, at] = lower[:, k * BLK : (k + 1) * BLK]

                @pl.when(row < 2)
                def _():
                    block = solved[:, k * BLK : (k + 1) * BLK]
                    top_ref[:, at] = jnp.where(row == 0, block[:BLK], block[BLK:])

    at = pl.ds(pl.multiple_of(step * rows, rows), rows)
    solved_rows = s_ref[at, :]
    shigh, slow = halves(solved_rows)
    wide = jnp.concatenate([shigh, shigh, slow], 1)
    for n in range(8):
        cut = slice(n * 256, (n + 1) * 256)
        thigh, tlow = thigh_ref[:, cut], tlow_ref[:, cut]
        sum_ref[:, cut] = dot(wide, jnp.concatenate([thigh, tlow, thigh], 0), ((1,), (0,)))
    o_ref[...] = a_ref[...] - sum_ref[...].reshape(rows, 16, BLK).reshape(rows * 16, BLK)

    @pl.when((row < 2) & (step == 0))
    def _():
        o_ref[: BLK * 16, :] = top_ref[...].reshape(BLK, 16, BLK).reshape(BLK * 16, BLK)

    @pl.when(col < 2)
    def _():
        o_ref[pl.ds(0, rows, 16), :] = jnp.where(
            col == 0, solved_rows[:, :BLK], solved_rows[:, BLK:]
        )

    @pl.when((row < 2) & (col < 2) & (step == 0))
    def _():
        strip = u_ref[pl.ds(pl.multiple_of(col * BLK, BLK), BLK), :]
        o_ref[pl.ds(0, BLK, 16), :] = jnp.where(row == 0, strip[:, :BLK], strip[:, BLK:]).T


def update(pos, a, early, mine, other, inverse, upper):
    rows = 2 * BLK
    vmem = pl.BlockSpec(memory_space=pltpu.VMEM)
    tile = pl.BlockSpec((rows * 16, BLK), lambda i: (i, 0))
    return pl.pallas_call(
        functools.partial(update_kernel, rows),
        grid=(512 // rows,),
        out_shape=jax.ShapeDtypeStruct(a.shape, jnp.float32),
        in_specs=[pl.BlockSpec(memory_space=pltpu.SMEM), tile] + [vmem] * 8,
        out_specs=tile,
        scratch_shapes=[
            pltpu.VMEM((PANEL, 2048), jnp.bfloat16),
            pltpu.VMEM((PANEL, 2048), jnp.bfloat16),
            pltpu.VMEM((BLK, 2048), jnp.float32),
            pltpu.VMEM((rows, 2048), jnp.float32),
        ],
        compiler_params=pltpu.CompilerParams(vmem_limit_bytes=40 * 1024 * 1024),
        cost_estimate=pl.CostEstimate(
            flops=3000000000, bytes_accessed=12000000, transcendentals=0
        ),
        name="update",
    )(pos, a, *early, mine, other, inverse, upper)


def local(kernel):
    row = lax.axis_index("row")
    col = lax.axis_index("col")
    zh, y, core = row // 8, (row // 2) % 4, row % 2
    zl, x = col // 4, col % 4
    low = (x == 0) | (x == 3)
    pos = jnp.stack([row, col, y, zh, core, low.astype(row.dtype)]).astype(jnp.int32)
    flat = kernel.reshape(512 * 16, BLK)
    left, p0, p1, p2, p3 = prepare(pos, flat)

    with jax.named_scope("rows"):
        held = spread(zl, left, [left], [lambda zh, y, core, zl, x: (zh, y, core, 1, x) if zl == 0 and x < 2 else None])
        near = spread(x >> 1, held, [held], [lambda zh, y, core, zl, x: (zh, y, core, zl, 3 - x) if x < 2 else None])

    with jax.named_scope("diag"):
        diag = left[:BLK]
        root = lambda zh, y, zl, x: (zh, y, zl) == (0, 0, 0) and x < 2
        stages = [
            [
                lambda zh, y, core, zl, x, t=t, m=m: (0, 0, core, t, 3 - x if m else x) if root(zh, y, zl, x) else None
                for t, m in ((0, True), (1, False), (1, True))
            ],
            [
                lambda zh, y, core, zl, x, s=s: (0, y + s, core, zl, x) if (zh, y) == (0, 0) else None
                for s in (1, 3, 2)
            ],
            [
                lambda zh, y, core, zl, x, s=s: (zh + s, y, core, zl, x) if zh == 0 else None
                for s in (1, 3, 2)
            ],
        ]
        near_pair = (x >> 1) + 2 * zl
        arrivals = [
            jnp.where((zh == 0) & (y == 0), near_pair, 0),
            jnp.where(zh == 0, jnp.where(y == 0, 0, jnp.where(y == 1, 1, jnp.where(y == 3, 2, 3))), 0),
            jnp.where(zh == 0, 0, jnp.where(zh == 1, 1, jnp.where(zh == 3, 2, 3))),
        ]
        for which, targets in zip(arrivals, stages):
            diag = spread(which, diag, [diag] * 3, targets)
        across = send(diag, lambda zh, y, core, zl, x: (zh, y, core, zl, x ^ 1))
        both = send(diag, lambda zh, y, core, zl, x: (zh, y, 1 - core, zl, x ^ 1))
        tied, near = lax.optimization_barrier((diag, near))
        cored = send(tied, lambda zh, y, core, zl, x: (zh, y, 1 - core, zl, x))
        far = send(near, lambda zh, y, core, zl, x: (zh, y, core, zl, x ^ 1))
        upper, inverse = factorize(pos, diag, across, cored, both)

    with jax.named_scope("cols"):
        piece = spread(
            lax.rem(y - (col >> 1) + 4, 4) + 1,
            None,
            [p0, p1, p2, p3],
            [
                lambda zh, y, core, zl, x, s=s: (zh, y + s, x, y // 2, 2 * (y % 2) + core)
                if zl == 0 and x < 2
                else None
                for s in range(4)
            ],
        )
        over_z = [piece] + [
            send(piece, lambda zh, y, core, zl, x, s=s: (zh - s, y, core, zl, x)) for s in (1, 2, 3)
        ]
        own = jnp.concatenate(over_z)
        halfway = send(own, lambda zh, y, core, zl, x: (zh, y - 2, core, zl, x))
        around = [
            send(own, lambda zh, y, core, zl, x: (zh, y - 1, core, zl, x)),
            halfway,
            send(own, lambda zh, y, core, zl, x: (zh, y - 3, core, zl, x)),
        ]
        swap = lambda zh, y, core, zl, x: (zh, y, 1 - core, zl, x)
        own_other = send(own, swap)
        up, down, inverse = lax.optimization_barrier((around[0], around[2], inverse))
        other = [own_other, send(up, swap), None, send(down, swap)]
        early = solve_early(pos, near, far, own, own_other, inverse)
        opposite, *early = lax.optimization_barrier((around[1], *early))
        other[2] = send(opposite, swap)
        sides = solve_sides(pos, up, other[1], down, other[3], inverse)

    with jax.named_scope("final"):
        out = update(pos, flat, [*early, *sides], opposite, other[2], inverse, upper)
    return out.reshape(kernel.shape)


def solution(mesh):
    placed = P(None, "row", None, None, "col", None)
    return jax.shard_map(
        local, mesh=mesh, in_specs=(placed,), out_specs=placed, check_vma=False
    )
```
